1024 devices in a mesh: grp: 64 (over z, y_lo), mem: 16 (over y_hi, x, core).
Axes of the slice: x: 4, y: 8 (y_hi: 2, y_lo: 4; y = y_hi * 4 + y_lo), z: 16, core: 2. Of those that a mesh axis runs over, the one named last changes fastest.
Arguments:
- student: bfloat16 [196608, 512], P(('grp', 'mem')), may hold values from -6 to 6
- teacher: bfloat16 [196608, 1280], P(('grp', 'mem')), may hold values from -6 to 6
- block_target: float32 [196608, 3072], P(('grp', 'mem')), may hold values from -1 to 1
Outputs:
- student_grad: float32 [196608, 512], P(('grp', 'mem'))
The draws below stay inside these ranges and needn't reach their ends.
All inputs are finite; a program needn't handle non-finite values.
Results may differ from the reference program's by a relative error of at most 0.0031.
Values may be sent and summed in bfloat16 or wider, within the bound.
A program may use at most 32 MiB of HBM per device.

```python
import math
import jax
import jax.numpy as jnp
from jax import lax

DS = 512
DT = 1280
ROWS_DEV = 192
REACH = 3
BLOCK = 3072
BATCH = 196608
N_GRP = 64
N_MEM = 16


def steps_of(own_key, shape, pieces, smallest, top_value):
    def one(axis_at, blocks):
        draws = jax.random.uniform(jax.random.fold_in(jax.random.fold_in(own_key, 6), axis_at), (blocks,), jnp.float32, smallest / len(pieces), top_value / len(pieces))
        return jnp.repeat(jnp.exp(draws), shape[axis_at] // blocks).reshape((-1,) + (1,) * (len(shape) - axis_at - 1))

    level = one(*pieces[0])
    for cut in pieces[1:]:
        level = level * one(*cut)
    return level


def scatter_about(rng, dims, deviation, limit, shards=(), dtype=jnp.bfloat16):
    entries = deviation * jax.random.normal(rng, dims, jnp.float32)
    if shards:
        entries = entries * steps_of(rng, dims, shards, -0.22, 0.18)
    return jnp.clip(entries, -limit, limit).astype(dtype)


def setup_inputs(seed: int = 0) -> dict:
    streams_of = jax.random.split(jax.random.key(seed), 4)
    student = scatter_about(streams_of[0], (BATCH, DS), 1.0, 6.0, ((0, 1024),))
    teacher = scatter_about(streams_of[1], (BATCH, DT), 1.0, 6.0, ((0, 1024),))
    block_target = scatter_about(streams_of[2], (BATCH, BLOCK), (1.5 / DS ** 0.5), 1.0, ((0, 1024),), jnp.float32)
    return {"student": student, "teacher": teacher, "block_target": block_target}


def normalize(values):
    wide = values.astype(jnp.float32)
    return (wide * lax.rsqrt(lax.optimization_barrier(jnp.sum(wide * wide, axis=1, keepdims=True)) + 1e-06)).astype(jnp.bfloat16)

def reference(student, teacher, block_target):
    snorm = normalize(student)
    tnorm = normalize(teacher)
    groups = N_GRP
    block_rows = ROWS_DEV * N_MEM
    swidth = snorm.shape[1]
    weight = 16.0 * math.sqrt(swidth / block_rows)
    contract = (((1,), (1,)), ((), ()))
    sgroups = snorm.reshape(groups, block_rows, swidth)
    targets = block_target.reshape(groups, block_rows, block_rows)

    def one_group(pair):
        sblock, target = pair
        inner = lax.dot_general(sblock, sblock, contract, preferred_element_type=jnp.float32) - target
        return jnp.dot(inner, sblock.astype(jnp.float32), precision=lax.Precision.HIGHEST)
    grad = lax.map(one_group, (sgroups, targets)).reshape(groups, N_MEM, ROWS_DEV, swidth)
    sfour = snorm.astype(jnp.float32).reshape(groups, N_MEM, ROWS_DEV, swidth)
    tfour = tnorm.astype(jnp.float32).reshape(groups, N_MEM, ROWS_DEV, tnorm.shape[1])
    high = lax.Precision.HIGHEST
    for reach_step in range(1, REACH + 1):
        for offset in (reach_step, -reach_step):
            spart = jnp.roll(sfour, -offset, axis=0)
            tpart = jnp.roll(tfour, -offset, axis=0)
            cross = jnp.einsum('gmrd,gmqd->gmrq', sfour, spart, precision=high) - jnp.einsum('gmrd,gmqd->gmrq', tfour, tpart, precision=high)
            grad = grad + jnp.einsum('gmrq,gmqd->gmrd', cross, spart, precision=high)
    return grad.reshape(snorm.shape[0], swidth) * weight
```

```python
import math

import jax
import jax.numpy as jnp
from jax import lax
from jax.experimental import pallas as pl
from jax.experimental.pallas import tpu as pltpu
from jax.sharding import PartitionSpec as P

MESH = pl.DeviceIdType.MESH
NX, NY, NZ, LINE = 4, 8, 16, 4
F32, BF16 = jnp.float32, jnp.bfloat16

CHAIN, XO, XQ, SIB = 0, 4, 7, 10
TLINE, SRIGHT = 18, 22
ZS, ZT, WS, WT, PZ, PF = 23, 27, 31, 32, 33, 37
COPIES = 41
RIGHT, LEFT, TWO, ZUP, ZDOWN, XUP, XDOWN, XTWO, CORE = range(9)
BACK = (LEFT, RIGHT, TWO, ZDOWN, ZUP, XDOWN, XUP, XTWO, CORE)
HOPS = (1, 3, 2)


def dot_t(a, b):
    return lax.dot_general(a, b, (((1,), (1,)), ((), ())), preferred_element_type=F32)


def t_dot(a, b):
    return lax.dot_general(a, b, (((0,), (0,)), ((), ())), preferred_element_type=F32)


def normalize(values):
    wide = values.astype(F32)
    return (wide * lax.rsqrt(jnp.sum(wide * wide, axis=1, keepdims=True) + 1e-06)).astype(BF16)


def kernel(
    student, teacher, target, out,
    blk, sp, tp, sq, tq, pin, pz, pzo, po, pacc, tgt, acc, ready, ssem, rsem, lsem,
):
    grp, mem = lax.axis_index("grp"), lax.axis_index("mem")
    z, a = grp // LINE, grp % LINE
    r, x, c = mem // 8, (mem // 2) % NX, mem % 2
    y = r * LINE + a
    way = 1 - 2 * c
    p = a + c * (3 - 2 * a)
    a_meet = 2 - c
    a_of = lambda place: place + c * (3 - 2 * place)
    meet = p == 2
    first_z, last_z = z == 0, z == NZ - 1
    rows = sp.shape[1]

    def at(dz=0, dy=0, dx=0, dc=0):
        yy, zz, xx = (y + dy + NY) % NY, (z + dz + NZ) % NZ, (x + dx) % NX
        cc = (c + dc) % 2
        rank = ((zz * NY + yy) * NX + xx) * 2 + cc
        rank = jnp.where(rank == 0, 2 * NX * NY * NZ, rank)
        return (zz * LINE + yy % LINE, (yy // LINE) * 8 + xx * 2 + cc), rank

    _, my_rank = at()
    two = jnp.where(p == 0, 2, -2) * way
    near = [at(dy=way), at(dy=-way), at(dy=two), at(dz=1), at(dz=-1), at(dx=1), at(dx=3), at(dx=2), at(dc=1)]
    used = [None, None, (p == 0) | (p == 2)] + [None] * 6
    earlier = [rank < my_rank for _, rank in near]
    dev = [d for d, _ in near]

    def over(n, cond):
        return cond if used[n] is None else cond & used[n]

    barrier = pltpu.get_barrier_semaphore()
    for n in range(9):
        @pl.when(over(n, jnp.logical_not(earlier[n])))
        def _():
            pl.semaphore_signal(barrier, 1, device_id=dev[n], device_id_type=MESH)

    load = pltpu.make_async_copy(target, tgt, lsem)
    load.start()
    me = r * 8 + x * 2 + c
    partner = (1 - r) * 8 + x * 2 + c
    own = normalize(student[...])
    sp[a] = own
    blk[me] = own
    tp[a] = normalize(teacher[...])

    peers = sum(over(n, earlier[n]).astype(jnp.int32) for n in range(9))
    @pl.when(peers > 0)
    def _():
        pl.semaphore_wait(barrier, peers)

    for n in range(9):
        @pl.when(over(n, earlier[n]))
        def _():
            pl.semaphore_signal(ready.at[BACK[n]], 1, device_id=dev[n], device_id_type=MESH)

    def wait_ready(n, cond=None):
        here = jnp.logical_not(earlier[n])
        here = over(n, here if cond is None else here & cond)
        @pl.when(here)
        def _():
            pl.semaphore_wait(ready.at[n], 1)

    started = []

    def send(i, src, dst, n, cond=None):
        copy = pltpu.make_async_remote_copy(
            src_ref=src, dst_ref=dst, send_sem=ssem.at[i], recv_sem=rsem.at[i],
            device_id=dev[n], device_id_type=MESH,
        )
        started.append((copy, cond))
        if cond is None:
            copy.start()
        else:
            pl.when(cond)(copy.start)

    def recv(i, dst, cond=None):
        copy = pltpu.make_async_remote_copy(
            src_ref=dst, dst_ref=dst, send_sem=ssem.at[i], recv_sem=rsem.at[i],
            device_id=dev[RIGHT], device_id_type=MESH,
        )
        if cond is None:
            copy.wait_recv()
        else:
            pl.when(cond)(copy.wait_recv)

    def chain_slot(d):
        yo = (y - d * way + NY) % NY
        return yo % LINE, (yo // LINE) * 8 + x * 2 + c

    def chain_send(d):
        ao, mo = chain_slot(d)
        src = sp.at[4] if d == 3 else sp.at[ao]
        dst = sp.at[ao] if d < 2 else sp.at[4] if d == 2 else blk.at[mo]
        send(CHAIN + d, src, dst, RIGHT)

    def chain_recv(d):
        ao, mo = chain_slot(d)
        recv(CHAIN + d - 1, sp.at[ao] if d < 3 else sp.at[4] if d == 3 else blk.at[mo])

    def x_send(base, whose):
        for k, n in enumerate((XUP, XDOWN, XTWO)):
            send(base + k, blk.at[whose], blk.at[whose], n)

    def sib_send(i, whose):
        send(SIB + i, blk.at[whose], blk.at[whose], CORE)

    def x_recv(base, part, sib):
        for k in range(3):
            whose = part * 8 + ((x + NX - HOPS[k]) % NX) * 2 + c
            recv(base + k, blk.at[whose])
            sib_send(sib + 1 + k, whose)

    def sib_recv(part, sib):
        for k in range(4):
            xx = x if k == 0 else (x + NX - HOPS[k - 1]) % NX
            recv(SIB + sib + k, blk.at[part * 8 + xx * 2 + 1 - c])

    def inner(part):
        def step(k, _):
            chip = part * 4 + k
            pair = jnp.concatenate([blk[2 * chip], blk[2 * chip + 1]], axis=0)
            cols = pl.ds(pl.multiple_of(chip * 2 * rows, 128), 2 * rows)
            affinity = dot_t(sp[a], pair) - tgt[:, cols]
            acc[...] += jnp.dot(affinity.astype(BF16), pair, preferred_element_type=F32)
            return 0

        lax.fori_loop(0, 4, step, 0)

    wait_ready(LEFT, p == 3)
    send(SRIGHT, sp.at[a], sp.at[a], LEFT, p == 3)
    send(TLINE + 3, tp.at[a], tp.at[a], LEFT, p == 3)
    wait_ready(RIGHT)
    chain_send(0)
    send(TLINE + 1, tp.at[a], tp.at[a], RIGHT, p == 1)
    wait_ready(TWO, p == 0)
    send(TLINE + 0, tp.at[a], tp.at[a], TWO, p == 0)
    wrap_out = last_z & jnp.logical_not(meet) & (a > 0)
    wrap_in = first_z & jnp.logical_not(meet) & (a > 0)
    up_now = meet | wrap_out
    forward = meet & jnp.logical_not(last_z)
    wait_ready(ZUP, up_now)
    send(ZS, sp.at[a], sq.at[a], ZUP, meet)
    send(ZT, tp.at[a], tq.at[a], ZUP, meet)
    send(WS, sp.at[a], sq.at[a], ZUP, wrap_out)
    send(WT, tp.at[a], tq.at[a], ZUP, wrap_out)
    wait_ready(CORE)
    sib_send(0, me)
    for n in (XUP, XDOWN, XTWO):
        wait_ready(n)
    x_send(XO, me)

    a_next, a_last = 3 - a_meet, 3
    chain_recv(1)
    chain_send(1)
    send(ZS + 1, sp.at[a_next], sq.at[a_next], ZUP, forward)
    chain_recv(2)
    chain_send(2)
    send(ZS + 2, sp.at[a_last], sq.at[a_last], ZUP, forward & (c == 1))
    recv(TLINE + 1, tp.at[a_next], meet)
    send(ZT + 1, tp.at[a_next], tq.at[a_next], ZUP, forward)
    x_recv(XO, r, 0)
    chain_recv(3)
    chain_send(3)
    recv(SRIGHT, sp.at[a_of(3)], meet)
    send(ZS + 2, sp.at[a_last], sq.at[a_last], ZUP, forward & (c == 0))
    recv(TLINE + 3, tp.at[a_of(3)], meet)
    send(ZT + 2, tp.at[a_last], tq.at[a_last], ZUP, forward & (c == 0))
    recv(TLINE + 0, tp.at[a_of(0)], meet)
    send(ZT + 2, tp.at[a_last], tq.at[a_last], ZUP, forward & (c == 1))

    @pl.when(meet)
    def _():
        pacc[...] = jnp.zeros_like(pacc)

        def outer(j, _):
            def step(i, _):
                cross = (dot_t(sp[i], sp[j]) - dot_t(tp[i], tp[j])).astype(BF16)
                pacc[i] += jnp.dot(cross, sp[j], preferred_element_type=F32)
                pacc[j] += t_dot(cross, sp[i])
                return 0

            return lax.fori_loop(0, j, step, 0)

        lax.fori_loop(1, LINE, outer, 0)

    chain_recv(4)
    sib_send(4, partner)
    x_send(XQ, partner)

    def across(i):
        acc[...] = jnp.zeros_like(acc)

        def step(j, _):
            cross = (dot_t(sq[i], sp[j]) - dot_t(tq[i], tp[j])).astype(BF16)
            acc[...] += jnp.dot(cross, sp[j], preferred_element_type=F32)
            pacc[j] += t_dot(cross, sq[i])
            return 0

        lax.fori_loop(0, i, step, 0)
        pzo[i] = acc[...].astype(BF16)

    def across_at(k, i):
        recv(ZS + k, sq.at[i], meet)
        recv(ZT + k, tq.at[i], meet)
        pl.when(meet)(lambda: across(i))
        send(PZ + k, pzo.at[i], pz.at[i], ZDOWN, meet)

    wait_ready(ZDOWN, meet)
    across_at(0, a_meet)
    across_at(1, a_next)

    recv(WS, sq.at[a], wrap_in)
    recv(WT, tq.at[a], wrap_in)
    seam_left = wrap_in & (p == 3)
    seam_right = wrap_in & (p == 1)
    seam_two = wrap_in & (p == 0)
    for i, buf in ((ZS, sq), (ZT, tq)):
        send(i + 2, buf.at[a], buf.at[a], LEFT, seam_left)
        send(i + 1, buf.at[a], buf.at[a], RIGHT, seam_right)
        send(i + 2, buf.at[a], buf.at[a], TWO, seam_two)

    x_recv(XQ, 1 - r, 4)
    across_at(2, a_last)

    wait_ready(LEFT, meet)
    wait_ready(TWO, meet)
    for k, i in enumerate((a_meet, a_next, a_last)):
        recv(PZ + k, pz.at[i], meet)

    @pl.when(meet)
    def _():
        for i in range(1, LINE):
            pacc[i] += pz[i].astype(F32)
        po[...] = pacc[...].astype(BF16)

    for place, n in ((0, TWO), (1, LEFT), (3, RIGHT)):
        send(PF + place, po.at[a_of(place)], pin, n, meet)

    acc[...] = jnp.zeros_like(acc)
    load.wait()
    sib_recv(r, 0)
    inner(r)
    sib_recv(1 - r, 4)
    inner(1 - r)

    @pl.when(meet)
    def _():
        out[...] = acc[...] + pacc[a]

    for place in (0, 1, 3):
        recv(PF + place, pin, p == place)

    @pl.when(jnp.logical_not(meet))
    def _():
        out[...] = acc[...] + pin[...].astype(F32)

    wait_ready(LEFT, (p == 0) | (p == 1))
    wait_ready(ZUP, jnp.logical_not(up_now))
    wait_ready(ZDOWN, jnp.logical_not(meet))
    for copy, cond in started:
        if cond is None:
            copy.wait_send()
        else:
            pl.when(cond)(copy.wait_send)


def body(student, teacher, block_target):
    rows, ds = student.shape
    dt = teacher.shape[1]
    columns = block_target.shape[1]
    weight = 16.0 * math.sqrt(ds / columns)
    vmem = pl.BlockSpec(memory_space=pltpu.VMEM)
    part = pl.pallas_call(
        kernel,
        out_shape=jax.ShapeDtypeStruct((rows, ds), F32),
        in_specs=[vmem, vmem, pl.BlockSpec(memory_space=pl.ANY)],
        out_specs=vmem,
        scratch_shapes=[
            pltpu.VMEM((16, rows, ds), BF16),
            pltpu.VMEM((5, rows, ds), BF16),
            pltpu.VMEM((4, rows, dt), BF16),
            pltpu.VMEM((4, rows, ds), BF16),
            pltpu.VMEM((4, rows, dt), BF16),
            pltpu.VMEM((rows, ds), BF16),
            pltpu.VMEM((4, rows, ds), BF16),
            pltpu.VMEM((4, rows, ds), BF16),
            pltpu.VMEM((4, rows, ds), BF16),
            pltpu.VMEM((4, rows, ds), F32),
            pltpu.VMEM((rows, columns), F32),
            pltpu.VMEM((rows, ds), F32),
            pltpu.SemaphoreType.REGULAR((9,)),
            pltpu.SemaphoreType.DMA((COPIES,)),
            pltpu.SemaphoreType.DMA((COPIES,)),
            pltpu.SemaphoreType.DMA,
        ],
        compiler_params=pltpu.CompilerParams(
            collective_id=0, has_side_effects=True, vmem_limit_bytes=48 * 2**20
        ),
    )(student, teacher, block_target)
    return part * weight


def solution(mesh):
    spec = P(("grp", "mem"), None)
    return jax.shard_map(body, mesh=mesh, in_specs=(spec,) * 3, out_specs=spec, check_vma=False)
```

```python
import math

import jax
import jax.numpy as jnp
from jax import lax
from jax.experimental import pallas as pl
from jax.experimental.pallas import tpu as pltpu
from jax.sharding import PartitionSpec as P

MESH = pl.DeviceIdType.MESH
NX, NY, NZ, LINE = 4, 8, 16, 4
F32, BF16 = jnp.float32, jnp.bfloat16

XO, XQ, FAR, SIB, SIBQ = 0, 3, 9, 11, 15
SLINE, TLINE = 23, 27
ZS, ZT, WS, WT, RT, PZ, PF = 31, 34, 37, 38, 42, 46, 49
COPIES = 53
RIGHT, LEFT, TWO, HALF, ZUP, ZDOWN, XUP, XDOWN, XTWO, CORE, DNEXT, DLAST, UPMEET = range(13)
BACK = (LEFT, RIGHT, TWO, HALF, ZDOWN, ZUP, XDOWN, XUP, XTWO, CORE, UPMEET, UPMEET, None)
HOPS = (1, 3, 2)
PIECES = 4
PARTS = 2


def dot_t(a, b):
    return lax.dot_general(a, b, (((1,), (1,)), ((), ())), preferred_element_type=F32)


def t_dot(a, b):
    return lax.dot_general(a, b, (((0,), (0,)), ((), ())), preferred_element_type=F32)


def normalize(values):
    wide = values.astype(F32)
    return (wide * lax.rsqrt(jnp.sum(wide * wide, axis=1, keepdims=True) + 1e-06)).astype(BF16)


def kernel(
    student, teacher, target, out,
    raw_s, raw_t, blk, sp, tp, sq, tq, pin, pin2, pzo, po, pacc, tgt, acc, ready, turn, ssem, rsem, lsem,
):
    grp, mem = lax.axis_index("grp"), lax.axis_index("mem")
    z, a = grp // LINE, grp % LINE
    r, x, c = mem // 8, (mem // 2) % NX, mem % 2
    y = r * LINE + a
    way = 1 - 2 * c
    p = a + c * (3 - 2 * a)
    a_meet = 2 - c
    a_of = lambda place: place + c * (3 - 2 * place)
    meet = p == 2
    first_z, last_z = z == 0, z == NZ - 1
    rows = sp.shape[1]

    def at(dz=0, dy=0, dx=0, dc=0):
        yy, zz, xx = (y + dy + NY) % NY, (z + dz + NZ) % NZ, (x + dx) % NX
        cc = (c + dc) % 2
        rank = ((zz * NY + yy) * NX + xx) * 2 + cc
        rank = jnp.where(rank == 0, 2 * NX * NY * NZ, rank)
        return (zz * LINE + yy % LINE, (yy // LINE) * 8 + xx * 2 + cc), rank

    _, my_rank = at()
    two = jnp.where(p == 0, 2, -2) * way
    near = [
        at(dy=way), at(dy=-way), at(dy=two), at(dy=4), at(dz=1), at(dz=-1), at(dx=1), at(dx=3), at(dx=2), at(dc=1),
        at(dz=-1, dy=-way), at(dz=-1, dy=jnp.where(c == 0, way, -2 * way)),
        at(dz=1, dy=jnp.where(p == 1, way, jnp.where(p == 3, -way, 2 * way))),
    ]
    wrap_out = last_z & jnp.logical_not(meet) & (a > 0)
    wrap_in = first_z & jnp.logical_not(meet) & (a > 0)
    forward = meet & jnp.logical_not(last_z)
    used = [p < 3, p > 0, (p == 0) | meet, None, meet | wrap_out, meet | wrap_in] + [None] * 4 + [meet, meet, (p == 1) | (a == 3)]
    earlier = [rank < my_rank for _, rank in near]
    dev = [d for d, _ in near]

    def over(n, cond):
        return cond if used[n] is None else cond & used[n]

    loads = [
        pltpu.make_async_copy(src, dst, lsem.at[k])
        for k, (src, dst) in enumerate(((student, raw_s), (teacher, raw_t), (target, tgt)))
    ]
    for load in loads:
        load.start()
    barrier = pltpu.get_barrier_semaphore()
    for n in range(13):
        @pl.when(over(n, jnp.logical_not(earlier[n])))
        def _():
            pl.semaphore_signal(barrier, 1, device_id=dev[n], device_id_type=MESH)

    me = r * 8 + x * 2 + c
    partner = (1 - r) * 8 + x * 2 + c
    peers = sum(over(n, earlier[n]).astype(jnp.int32) for n in range(13))
    @pl.when(peers > 0)
    def _():
        pl.semaphore_wait(barrier, peers)

    for n in range(13):
        @pl.when(over(n, earlier[n]))
        def _():
            pl.semaphore_signal(ready.at[jnp.where(p == 1, DNEXT, DLAST) if n == UPMEET else BACK[n]], 1, device_id=dev[n], device_id_type=MESH)

    loads[0].wait()
    own = normalize(raw_s[...])
    sp[a] = own
    blk[me] = own

    def wait_ready(n, cond=None):
        here = jnp.logical_not(earlier[n])
        here = over(n, here if cond is None else here & cond)
        @pl.when(here)
        def _():
            pl.semaphore_wait(ready.at[n], 1)

    started = []

    def send(i, src, dst, n, cond=None, end=None):
        copy = pltpu.make_async_remote_copy(
            src_ref=src, dst_ref=dst, send_sem=ssem.at[i], recv_sem=rsem.at[i if end is None else end],
            device_id=dev[n], device_id_type=MESH,
        )
        started.append((copy, cond))
        if cond is None:
            copy.start()
        else:
            pl.when(cond)(copy.start)

    def recv(i, dst, cond=None):
        copy = pltpu.make_async_remote_copy(
            src_ref=dst, dst_ref=dst, send_sem=ssem.at[i], recv_sem=rsem.at[i],
            device_id=dev[RIGHT], device_id_type=MESH,
        )
        if cond is None:
            copy.wait_recv()
        else:
            pl.when(cond)(copy.wait_recv)

    halves = [pl.ds(h * (rows // PARTS), rows // PARTS) for h in range(PARTS)]

    def half_of(whose, h):
        return blk.at[whose] if h is None else blk.at[whose, halves[h]]

    def x_send(base, whose, h=None, cond=None):
        for k, n in enumerate((XUP, XDOWN, XTWO)):
            send(base + k, half_of(whose, h), half_of(whose, h), n, cond)

    def sib_send(i, whose, h=None, cond=None):
        send(i, half_of(whose, h), half_of(whose, h), CORE, cond)

    def x_recv(base, part, sib, h=None, cond=None):
        for k in range(3):
            whose = part * 8 + ((x + NX - HOPS[k]) % NX) * 2 + c
            recv(base + k, half_of(whose, h), cond)
            sib_send(sib + 1 + k, whose, h, cond)

    def xq_recv(cond):
        for h in range(PARTS):
            x_recv(XQ + 3 * h, 1 - r, SIBQ + 4 * h, h, cond)

    def inner(part, whole):
        for k in range(4):
            xx = x if k == 0 else (x + NX - HOPS[k - 1]) % NX
            chip = part * 4 + xx
            if whole:
                recv(SIB + k, blk.at[2 * chip + 1 - c])
            else:
                for h in range(PARTS):
                    recv(SIBQ + 4 * h + k, half_of(2 * chip + 1 - c, h))
            pair = jnp.concatenate([blk[2 * chip], blk[2 * chip + 1]], axis=0)
            cols = pl.ds(pl.multiple_of(chip * 2 * rows, 128), 2 * rows)
            affinity = dot_t(sp[a], pair) - tgt[:, cols]
            acc[...] += jnp.dot(affinity.astype(BF16), pair, preferred_element_type=F32)

    ends = ((p == 3, LEFT, 3), (p == 1, RIGHT, 1), (p == 0, TWO, 0))
    wait_ready(ZUP, meet | wrap_out)
    send(WS, sp.at[a], sq.at[a], ZUP, wrap_out)
    for here, n, place in ends:
        wait_ready(n, here)
        send(SLINE + place, sp.at[a], sp.at[a], n, here)
    send(ZS, sp.at[a], sq.at[a], ZUP, meet)

    def far_send(cond):
        wait_ready(HALF, cond)
        for h in range(PARTS):
            send(FAR + h, half_of(me, h), half_of(me, h), HALF, cond)

    later = jnp.logical_not(first_z)
    loads[1].wait()
    tp[a] = normalize(raw_t[...])
    pieces = [pl.ds(k * (rows // PIECES), rows // PIECES) for k in range(PIECES)]
    for k, piece in enumerate(pieces):
        send(WT + k, tp.at[a, piece], tq.at[a, piece], ZUP, wrap_out)
    for here, n, place in ends[:2]:
        send(TLINE + place, tp.at[a], tp.at[a], n, here)
    ahead, third = len(started) - 1, len(started) - 2
    send(ZT, tp.at[a], tq.at[a], ZUP, meet)
    far_send(first_z)
    wait_ready(CORE)
    sib_send(SIB, me)
    for n in (XUP, XDOWN, XTWO):
        wait_ready(n)
    x_send(XO, me)

    wait_ready(RIGHT, p == 0)
    wait_ready(LEFT, p == 1)

    @pl.when(p == 1)
    def _():
        started[ahead][0].wait_send()
        pl.semaphore_signal(turn, 1, device_id=dev[LEFT], device_id_type=MESH)

    @pl.when(p == 0)
    def _():
        pl.semaphore_wait(turn, 1)

    send(TLINE + 0, tp.at[a], tp.at[a], TWO, p == 0)

    @pl.when(p == 3)
    def _():
        started[third][0].wait_send()

    far_send(later & jnp.logical_not(meet))

    a_next, a_last = 3 - a_meet, 3
    recv(SLINE + 1, sp.at[a_next], meet)
    send(ZS + 1, sp.at[a_next], sq.at[a_next], ZUP, forward)
    recv(TLINE + 1, tp.at[a_next], meet)
    send(ZT + 1, tp.at[a_next], tq.at[a_next], ZUP, forward)
    far_send(later & meet)
    x_recv(XO, r, SIB)
    def take(place, core):
        ap = a_of(place)
        recv(SLINE + place, sp.at[ap], meet)
        send(ZS + 2, sp.at[a_last], sq.at[a_last], ZUP, forward & (c == core))
        recv(TLINE + place, tp.at[ap], meet)
        send(ZT + 2, tp.at[a_last], tq.at[a_last], ZUP, forward & (c == core))

    def join(lo, hi, s_ref, t_ref):
        flat = lambda ref: ref[lo:hi].reshape((hi - lo) * rows, ref.shape[2])
        cross = (dot_t(flat(sp), s_ref[...]) - dot_t(flat(tp), t_ref[...])).astype(BF16)
        theirs = jnp.dot(cross, s_ref[...], preferred_element_type=F32)
        pacc[lo:hi] += theirs.reshape(hi - lo, rows, theirs.shape[1])
        return t_dot(cross, flat(sp))

    def joins(core, *steps):
        @pl.when(meet & (c == core))
        def _():
            for j, lo, hi in steps:
                pacc[j] += join(lo, hi, sp.at[j], tp.at[j])

    take(3, 0)
    pl.when(meet)(lambda: pacc.__setitem__(..., jnp.zeros_like(pacc)))
    joins(0, (2, 1, 2), (3, 1, 3))
    joins(1, (1, 0, 1), (2, 0, 2))
    acc[...] = jnp.zeros_like(acc)
    loads[2].wait()
    inner(r, True)
    take(0, 1)
    joins(0, (0, 1, 4))
    joins(1, (3, 0, 3))

    def give(place, n, cond):
        i = a_of(place)
        pl.when(cond)(lambda: po.__setitem__(i, pacc[i].astype(BF16)))
        send(PF + place, po.at[i], pin, n, cond)

    for n in (LEFT, RIGHT, TWO):
        wait_ready(n, meet)
    give(3, RIGHT, meet & (c == 0))
    give(0, TWO, meet & (c == 1))

    def far_recv(cond):
        for h in range(PARTS):
            recv(FAR + h, half_of(partner, h), cond)
            sib_send(SIBQ + 4 * h, partner, h, cond)
            x_send(XQ + 3 * h, partner, h, cond)

    def across(k, i, places):
        recv(ZS + k, sq.at[i], meet)
        recv(ZT + k, tq.at[i], meet)
        for n in places:
            @pl.when(meet & (i == n))
            def _():
                pzo[n] = join(0, n, sq.at[n], tq.at[n]).astype(BF16)
        send(PZ + k, pzo.at[i], pin2, (ZDOWN, DNEXT, DLAST)[k], meet)

    busy = meet & later
    far_recv(jnp.logical_not(busy))
    xq_recv(meet & first_z)
    for n in (ZDOWN, DNEXT, DLAST):
        wait_ready(n, meet | wrap_in if n == ZDOWN else None)
    across(0, a_meet, (1, 2))
    across(1, a_next, (1, 2))
    far_recv(busy)

    lines = ((3, LEFT, 2), (1, RIGHT, 1), (0, TWO, 2))
    recv(WS, sq.at[a], wrap_in)
    for place, n, k in lines:
        send(ZS + k, sq.at[a], sq.at[a], n, wrap_in & (p == place))
    for q, piece in enumerate(pieces):
        recv(WT + q, tq.at[a, piece], wrap_in)
        for place, n, k in lines:
            send(RT + q, tq.at[a, piece], tq.at[a, piece], n, wrap_in & (p == place), ZT + k)

    xq_recv(jnp.logical_not(meet))
    across(2, a_last, (3,))

    give(0, TWO, meet & (c == 0))
    give(3, RIGHT, meet & (c == 1))
    give(1, LEFT, meet)

    xq_recv(meet & later)
    inner(1 - r, False)

    @pl.when(meet)
    def _():
        acc[...] += pacc[a]

    for place in (0, 1, 3):
        recv(PF + place, pin, p == place)

    @pl.when(jnp.logical_not(meet))
    def _():
        acc[...] += pin[...].astype(F32)

    wait_ready(UPMEET)
    for k, here in enumerate((meet, p == 1, a == 3)):
        recv(PZ + k, pin2, here)

    @pl.when(a > 0)
    def _():
        out[...] = acc[...] + pin2[...].astype(F32)

    @pl.when(a == 0)
    def _():
        out[...] = acc[...]

    for k, (copy, cond) in enumerate(started):
        if k in (ahead, third):
            continue
        if cond is None:
            copy.wait_send()
        else:
            pl.when(cond)(copy.wait_send)


def body(student, teacher, block_target):
    rows, ds = student.shape
    dt = teacher.shape[1]
    columns = block_target.shape[1]
    weight = 16.0 * math.sqrt(ds / columns)
    vmem = pl.BlockSpec(memory_space=pltpu.VMEM)
    part = pl.pallas_call(
        kernel,
        out_shape=jax.ShapeDtypeStruct((rows, ds), F32),
        in_specs=[pl.BlockSpec(memory_space=pltpu.HBM)] * 3,
        out_specs=vmem,
        scratch_shapes=[
            pltpu.VMEM((rows, ds), BF16),
            pltpu.VMEM((rows, dt), BF16),
            pltpu.VMEM((16, rows, ds), BF16),
            pltpu.VMEM((4, rows, ds), BF16),
            pltpu.VMEM((4, rows, dt), BF16),
            pltpu.VMEM((4, rows, ds), BF16),
            pltpu.VMEM((4, rows, dt), BF16),
            pltpu.VMEM((rows, ds), BF16),
            pltpu.VMEM((rows, ds), BF16),
            pltpu.VMEM((4, rows, ds), BF16),
            pltpu.VMEM((4, rows, ds), BF16),
            pltpu.VMEM((4, rows, ds), F32),
            pltpu.VMEM((rows, columns), F32),
            pltpu.VMEM((rows, ds), F32),
            pltpu.SemaphoreType.REGULAR((13,)),
            pltpu.SemaphoreType.REGULAR,
            pltpu.SemaphoreType.DMA((COPIES,)),
            pltpu.SemaphoreType.DMA((COPIES,)),
            pltpu.SemaphoreType.DMA((3,)),
        ],
        compiler_params=pltpu.CompilerParams(
            collective_id=0, has_side_effects=True, vmem_limit_bytes=62 * 2**20
        ),
    )(student, teacher, block_target)
    return part * weight


def solution(mesh):
    spec = P(("grp", "mem"), None)
    return jax.shard_map(body, mesh=mesh, in_specs=(spec,) * 3, out_specs=spec, check_vma=False)
```

```python
import math

import jax
import jax.numpy as jnp
from jax import lax
from jax.experimental import pallas as pl
from jax.experimental.pallas import tpu as pltpu
from jax.sharding import PartitionSpec as P

MESH = pl.DeviceIdType.MESH
NX, NY, NZ, LINE = 4, 8, 16, 4
F32, BF16 = jnp.float32, jnp.bfloat16

XO, XQ, FAR, SIB, SIBQ = 0, 3, 9, 11, 15
SLINE, TLINE = 23, 27
ZS, ZT, WS, WT, RT, PZ, PF = 31, 34, 37, 38, 42, 46, 49
COPIES = 53
RIGHT, LEFT, TWO, HALF, ZUP, ZDOWN, XUP, XDOWN, XTWO, CORE, DNEXT, DLAST, UPMEET = range(13)
BACK = (LEFT, RIGHT, TWO, HALF, ZDOWN, ZUP, XDOWN, XUP, XTWO, CORE, UPMEET, UPMEET, None)
HOPS = (1, 3, 2)
PIECES = 4
PARTS = 2


def dot_t(a, b):
    return lax.dot_general(a, b, (((1,), (1,)), ((), ())), preferred_element_type=F32)


def t_dot(a, b):
    return lax.dot_general(a, b, (((0,), (0,)), ((), ())), preferred_element_type=F32)


def normalize(values):
    wide = values.astype(F32)
    return (wide * lax.rsqrt(jnp.sum(wide * wide, axis=1, keepdims=True) + 1e-06)).astype(BF16)


def kernel(
    student, teacher, target, out,
    raw_s, raw_t, blk, sp, tp, sq, tq, pin, pin2, pzo, po, pacc, tgt, acc, ready, turn, ssem, rsem, lsem,
):
    grp, mem = lax.axis_index("grp"), lax.axis_index("mem")
    z, a = grp // LINE, grp % LINE
    r, x, c = mem // 8, (mem // 2) % NX, mem % 2
    y = r * LINE + a
    way = 1 - 2 * c
    p = a + c * (3 - 2 * a)
    a_meet = 2 - c
    a_of = lambda place: place + c * (3 - 2 * place)
    meet = p == 2
    first_z, last_z = z == 0, z == NZ - 1
    rows = sp.shape[1]

    def at(dz=0, dy=0, dx=0, dc=0):
        yy, zz, xx = (y + dy + NY) % NY, (z + dz + NZ) % NZ, (x + dx) % NX
        cc = (c + dc) % 2
        rank = ((zz * NY + yy) * NX + xx) * 2 + cc
        rank = jnp.where(rank == 0, 2 * NX * NY * NZ, rank)
        return (zz * LINE + yy % LINE, (yy // LINE) * 8 + xx * 2 + cc), rank

    _, my_rank = at()
    two = jnp.where(p == 0, 2, -2) * way
    near = [
        at(dy=way), at(dy=-way), at(dy=two), at(dy=4), at(dz=1), at(dz=-1), at(dx=1), at(dx=3), at(dx=2), at(dc=1),
        at(dz=-1, dy=-way), at(dz=-1, dy=jnp.where(c == 0, way, -2 * way)),
        at(dz=1, dy=jnp.where(p == 1, way, jnp.where(p == 3, -way, 2 * way))),
    ]
    wrap_out = last_z & jnp.logical_not(meet) & (a > 0)
    wrap_in = first_z & jnp.logical_not(meet) & (a > 0)
    forward = meet & jnp.logical_not(last_z)
    used = [p < 3, p > 0, (p == 0) | meet, None, meet | wrap_out, meet | wrap_in] + [None] * 4 + [meet, meet, (p == 1) | (a == 3)]
    earlier = [rank < my_rank for _, rank in near]
    dev = [d for d, _ in near]

    def over(n, cond):
        return cond if used[n] is None else cond & used[n]

    loads = [
        pltpu.make_async_copy(src, dst, lsem.at[k])
        for k, (src, dst) in enumerate(((student, raw_s), (teacher, raw_t), (target, tgt)))
    ]
    for load in loads:
        load.start()
    barrier = pltpu.get_barrier_semaphore()
    for n in range(13):
        @pl.when(over(n, jnp.logical_not(earlier[n])))
        def _():
            pl.semaphore_signal(barrier, 1, device_id=dev[n], device_id_type=MESH)

    me = r * 8 + x * 2 + c
    partner = (1 - r) * 8 + x * 2 + c
    peers = sum(over(n, earlier[n]).astype(jnp.int32) for n in range(13))
    @pl.when(peers > 0)
    def _():
        pl.semaphore_wait(barrier, peers)

    for n in range(13):
        @pl.when(over(n, earlier[n]))
        def _():
            pl.semaphore_signal(ready.at[jnp.where(p == 1, DNEXT, DLAST) if n == UPMEET else BACK[n]], 1, device_id=dev[n], device_id_type=MESH)

    loads[0].wait()
    own = normalize(raw_s[...])
    sp[a] = own
    blk[me] = own

    def wait_ready(n, cond=None):
        here = jnp.logical_not(earlier[n])
        here = over(n, here if cond is None else here & cond)
        @pl.when(here)
        def _():
            pl.semaphore_wait(ready.at[n], 1)

    started = []

    def send(i, src, dst, n, cond=None, end=None):
        copy = pltpu.make_async_remote_copy(
            src_ref=src, dst_ref=dst, send_sem=ssem.at[i], recv_sem=rsem.at[i if end is None else end],
            device_id=dev[n], device_id_type=MESH,
        )
        started.append((copy, cond))
        if cond is None:
            copy.start()
        else:
            pl.when(cond)(copy.start)

    def recv(i, dst, cond=None):
        copy = pltpu.make_async_remote_copy(
            src_ref=dst, dst_ref=dst, send_sem=ssem.at[i], recv_sem=rsem.at[i],
            device_id=dev[RIGHT], device_id_type=MESH,
        )
        if cond is None:
            copy.wait_recv()
        else:
            pl.when(cond)(copy.wait_recv)

    halves = [pl.ds(h * (rows // PARTS), rows // PARTS) for h in range(PARTS)]

    def half_of(whose, h):
        return blk.at[whose] if h is None else blk.at[whose, halves[h]]

    def x_send(base, whose, h=None, cond=None):
        for k, n in enumerate((XUP, XDOWN, XTWO)):
            send(base + k, half_of(whose, h), half_of(whose, h), n, cond)

    def sib_send(i, whose, h=None, cond=None):
        send(i, half_of(whose, h), half_of(whose, h), CORE, cond)

    def x_recv(base, part, sib, h=None, cond=None):
        for k in range(3):
            whose = part * 8 + ((x + NX - HOPS[k]) % NX) * 2 + c
            recv(base + k, half_of(whose, h), cond)
            sib_send(sib + 1 + k, whose, h, cond)

    def xq_recv(cond):
        for h in range(PARTS):
            x_recv(XQ + 3 * h, 1 - r, SIBQ + 4 * h, h, cond)

    def inner(part, whole):
        for k in range(4):
            xx = x if k == 0 else (x + NX - HOPS[k - 1]) % NX
            chip = part * 4 + xx
            if whole:
                recv(SIB + k, blk.at[2 * chip + 1 - c])
            else:
                for h in range(PARTS):
                    recv(SIBQ + 4 * h + k, half_of(2 * chip + 1 - c, h))
            pair = jnp.concatenate([blk[2 * chip], blk[2 * chip + 1]], axis=0)
            cols = pl.ds(pl.multiple_of(chip * 2 * rows, 128), 2 * rows)
            affinity = dot_t(sp[a], pair) - tgt[:, cols]
            acc[...] += jnp.dot(affinity.astype(BF16), pair, preferred_element_type=F32)

    ends = ((p == 3, LEFT, 3), (p == 1, RIGHT, 1), (p == 0, TWO, 0))
    wait_ready(ZUP, meet | wrap_out)
    send(WS, sp.at[a], sq.at[a], ZUP, wrap_out)
    for here, n, place in ends:
        wait_ready(n, here)
        send(SLINE + place, sp.at[a], sp.at[a], n, here)
    send(ZS, sp.at[a], sq.at[a], ZUP, meet)

    def far_send(cond):
        wait_ready(HALF, cond)
        for h in range(PARTS):
            send(FAR + h, half_of(me, h), half_of(me, h), HALF, cond)

    later = jnp.logical_not(first_z)
    loads[1].wait()
    tp[a] = normalize(raw_t[...])
    pieces = [pl.ds(k * (rows // PIECES), rows // PIECES) for k in range(PIECES)]
    for k, piece in enumerate(pieces):
        send(WT + k, tp.at[a, piece], tq.at[a, piece], ZUP, wrap_out)
    for here, n, place in ends[:2]:
        send(TLINE + place, tp.at[a], tp.at[a], n, here)
    ahead, third = len(started) - 1, len(started) - 2
    send(ZT, tp.at[a], tq.at[a], ZUP, meet)
    early = first_z & (a == 0)
    far_send(early)
    wait_ready(CORE)
    sib_send(SIB, me)
    for n in (XUP, XDOWN, XTWO):
        wait_ready(n)
    x_send(XO, me)

    wait_ready(RIGHT, p == 0)
    wait_ready(LEFT, p == 1)

    @pl.when(p == 1)
    def _():
        started[ahead][0].wait_send()
        pl.semaphore_signal(turn, 1, device_id=dev[LEFT], device_id_type=MESH)

    @pl.when(p == 0)
    def _():
        pl.semaphore_wait(turn, 1)

    send(TLINE + 0, tp.at[a], tp.at[a], TWO, p == 0)

    @pl.when(p == 3)
    def _():
        started[third][0].wait_send()

    far_send(jnp.logical_not(early | meet))

    a_next, a_last = 3 - a_meet, 3
    recv(SLINE + 1, sp.at[a_next], meet)
    send(ZS + 1, sp.at[a_next], sq.at[a_next], ZUP, forward)
    recv(TLINE + 1, tp.at[a_next], meet)
    send(ZT + 1, tp.at[a_next], tq.at[a_next], ZUP, forward)
    far_send(meet)
    x_recv(XO, r, SIB)
    def take(place, core):
        ap = a_of(place)
        recv(SLINE + place, sp.at[ap], meet)
        send(ZS + 2, sp.at[a_last], sq.at[a_last], ZUP, forward & (c == core))
        recv(TLINE + place, tp.at[ap], meet)
        send(ZT + 2, tp.at[a_last], tq.at[a_last], ZUP, forward & (c == core))

    def join(lo, hi, s_ref, t_ref):
        flat = lambda ref: ref[lo:hi].reshape((hi - lo) * rows, ref.shape[2])
        cross = (dot_t(flat(sp), s_ref[...]) - dot_t(flat(tp), t_ref[...])).astype(BF16)
        theirs = jnp.dot(cross, s_ref[...], preferred_element_type=F32)
        pacc[lo:hi] += theirs.reshape(hi - lo, rows, theirs.shape[1])
        return t_dot(cross, flat(sp))

    def joins(core, *steps):
        @pl.when(meet & (c == core))
        def _():
            for j, lo, hi in steps:
                pacc[j] += join(lo, hi, sp.at[j], tp.at[j])

    take(3, 0)
    pl.when(meet)(lambda: pacc.__setitem__(..., jnp.zeros_like(pacc)))
    joins(0, (2, 1, 2), (3, 1, 3))
    joins(1, (1, 0, 1), (2, 0, 2))
    acc[...] = jnp.zeros_like(acc)
    loads[2].wait()
    inner(r, True)
    take(0, 1)
    joins(0, (0, 1, 4))
    joins(1, (3, 0, 3))

    def give(place, n, cond):
        i = a_of(place)
        pl.when(cond)(lambda: po.__setitem__(i, pacc[i].astype(BF16)))
        send(PF + place, po.at[i], pin, n, cond)

    for n in (LEFT, RIGHT, TWO):
        wait_ready(n, meet)
    give(3, RIGHT, meet & (c == 0))
    give(0, TWO, meet & (c == 1))

    def far_recv(cond):
        for h in range(PARTS):
            recv(FAR + h, half_of(partner, h), cond)
            sib_send(SIBQ + 4 * h, partner, h, cond)
            x_send(XQ + 3 * h, partner, h, cond)

    def across(k, i, places):
        recv(ZS + k, sq.at[i], meet)
        recv(ZT + k, tq.at[i], meet)
        for n in places:
            @pl.when(meet & (i == n))
            def _():
                pzo[n] = join(0, n, sq.at[n], tq.at[n]).astype(BF16)
        send(PZ + k, pzo.at[i], pin2, (ZDOWN, DNEXT, DLAST)[k], meet)

    busy = meet & later
    far_recv(jnp.logical_not(busy))
    xq_recv(meet & first_z)
    for n in (ZDOWN, DNEXT, DLAST):
        wait_ready(n, meet | wrap_in if n == ZDOWN else None)
    across(0, a_meet, (1, 2))
    across(1, a_next, (1, 2))
    far_recv(busy)

    lines = ((3, LEFT, 2), (1, RIGHT, 1), (0, TWO, 2))
    recv(WS, sq.at[a], wrap_in)
    for place, n, k in lines:
        send(ZS + k, sq.at[a], sq.at[a], n, wrap_in & (p == place))
    for q, piece in enumerate(pieces):
        recv(WT + q, tq.at[a, piece], wrap_in)
        for place, n, k in lines:
            send(RT + q, tq.at[a, piece], tq.at[a, piece], n, wrap_in & (p == place), ZT + k)

    xq_recv(jnp.logical_not(meet))
    across(2, a_last, (3,))

    give(0, TWO, meet & (c == 0))
    give(3, RIGHT, meet & (c == 1))
    give(1, LEFT, meet)

    xq_recv(meet & later)
    inner(1 - r, False)

    @pl.when(meet)
    def _():
        acc[...] += pacc[a]

    for place in (0, 1, 3):
        recv(PF + place, pin, p == place)

    @pl.when(jnp.logical_not(meet))
    def _():
        acc[...] += pin[...].astype(F32)

    wait_ready(UPMEET)
    for k, here in enumerate((meet, p == 1, a == 3)):
        recv(PZ + k, pin2, here)

    @pl.when(a > 0)
    def _():
        out[...] = acc[...] + pin2[...].astype(F32)

    @pl.when(a == 0)
    def _():
        out[...] = acc[...]

    for k, (copy, cond) in enumerate(started):
        if k in (ahead, third):
            continue
        if cond is None:
            copy.wait_send()
        else:
            pl.when(cond)(copy.wait_send)


def body(student, teacher, block_target):
    rows, ds = student.shape
    dt = teacher.shape[1]
    columns = block_target.shape[1]
    weight = 16.0 * math.sqrt(ds / columns)
    vmem = pl.BlockSpec(memory_space=pltpu.VMEM)
    part = pl.pallas_call(
        kernel,
        out_shape=jax.ShapeDtypeStruct((rows, ds), F32),
        in_specs=[pl.BlockSpec(memory_space=pltpu.HBM)] * 3,
        out_specs=vmem,
        scratch_shapes=[
            pltpu.VMEM((rows, ds), BF16),
            pltpu.VMEM((rows, dt), BF16),
            pltpu.VMEM((16, rows, ds), BF16),
            pltpu.VMEM((4, rows, ds), BF16),
            pltpu.VMEM((4, rows, dt), BF16),
            pltpu.VMEM((4, rows, ds), BF16),
            pltpu.VMEM((4, rows, dt), BF16),
            pltpu.VMEM((rows, ds), BF16),
            pltpu.VMEM((rows, ds), BF16),
            pltpu.VMEM((4, rows, ds), BF16),
            pltpu.VMEM((4, rows, ds), BF16),
            pltpu.VMEM((4, rows, ds), F32),
            pltpu.VMEM((rows, columns), F32),
            pltpu.VMEM((rows, ds), F32),
            pltpu.SemaphoreType.REGULAR((13,)),
            pltpu.SemaphoreType.REGULAR,
            pltpu.SemaphoreType.DMA((COPIES,)),
            pltpu.SemaphoreType.DMA((COPIES,)),
            pltpu.SemaphoreType.DMA((3,)),
        ],
        compiler_params=pltpu.CompilerParams(
            collective_id=0, has_side_effects=True, vmem_limit_bytes=62 * 2**20
        ),
    )(student, teacher, block_target)
    return part * weight


def solution(mesh):
    spec = P(("grp", "mem"), None)
    return jax.shard_map(body, mesh=mesh, in_specs=(spec,) * 3, out_specs=spec, check_vma=False)
```
